128 devices in a mesh: ep: 8 (over z, core), etp: 4 (over y), dp: 4 (over x).
Axes of the slice: x: 4, y: 4, z: 4, core: 2. Of those that a mesh axis runs over, the one named last changes fastest.
Arguments:
- inputs: bfloat16 [32768, 4096], P(('ep', 'etp', 'dp')), may hold values from -6 to 6
- upstream: bfloat16 [32768, 4096], P(('ep', 'etp', 'dp')), may hold values from -24 to 24
- experts: int32 [32768, 8], P(('ep', 'etp', 'dp')), may hold values from 0 to 127, all different within a row
- gate_probs: float32 [32768, 8], P(('ep', 'etp', 'dp')), may hold values from 0.05 to 0.5
- gate_weight: bfloat16 [8, 4096, 1536], P('ep', None, 'etp'), may hold values from -0.09375 to 0.09375
- up_weight: bfloat16 [8, 4096, 1536], P('ep', None, 'etp'), may hold values from -0.09375 to 0.09375
- down_weight: bfloat16 [8, 1536, 4096], P('ep', 'etp'), may hold values from -0.15625 to 0.15625
Outputs:
- grad_inputs: bfloat16 [32768, 4096], P(('ep', 'etp', 'dp'))
- grad_probs: float32 [32768, 8], P(('ep', 'etp', 'dp'))
- grad_gate: bfloat16 [8, 4096, 1536], P('ep', 'dp', 'etp')
- grad_up: bfloat16 [8, 4096, 1536], P('ep', 'dp', 'etp')
- grad_down: bfloat16 [8, 1536, 4096], P('ep', 'etp', 'dp')
The draws below stay inside these ranges and needn't reach their ends.
All inputs are finite; a program needn't handle non-finite values.
Results may differ from the reference program's by a relative error of at most 0.013.
Values may be sent and summed in bfloat16 or wider, within the bound.
No kernel may reach another device: no remote copies, remote signals or barrier semaphores. Data moves between devices by JAX's collectives and lax.ppermute only.
A program may use at most 128 MiB of HBM per device.

```python
import math
import jax
import jax.numpy as jnp
from jax import lax

D = 4096
FF = 1536
EXPERTS = 128
TOP = 8
TOK_DEV = 256
CAP = 24
WINDOW = 8
PIECES = 4
GROUPS = 4
BLOCKS = 128
TOKENS = 32768


def block_levels(rng, shape, pieces, low, largest):
    level = 1.0
    for position, shards_of in pieces:
        steps = jax.random.uniform(jax.random.fold_in(jax.random.fold_in(rng, 6), position), (shards_of,), jnp.float32, low / len(pieces), largest / len(pieces))
        level = level * jnp.repeat(jnp.exp(steps), shape[position] // shards_of).reshape((-1,) + (1,) * (len(shape) - 1 - position))
    return level


def choose_distinct(stream_key, rows, number_of, top, lift):
    ranking = jax.random.permutation(jax.random.fold_in(stream_key, 1), number_of)
    pull = ranking
    for power in range(3):
        pull = pull * pull // number_of
    pull = pull * lift // number_of
    tickets = jax.random.randint(jax.random.fold_in(stream_key, 2), (rows, number_of), 0, 4096) + pull
    fixed_rows = jax.random.permutation(jax.random.fold_in(stream_key, 3), rows)[jnp.arange(number_of) % rows]
    tickets = jnp.where(jnp.arange(rows)[:, None] == fixed_rows[None, :], 1 << 14, tickets)
    score = tickets * number_of + jnp.arange(number_of)
    return lax.top_k(score.astype(jnp.int32), top)[1].astype(jnp.int32)


def normal_values(rng, extent, deviation, bound, shards=(), kind=jnp.bfloat16):
    gain = block_levels(rng, extent, shards, -0.22, 0.18) if shards else 1.0
    values = jax.random.normal(rng, extent, jnp.float32) * deviation * gain
    return jnp.minimum(jnp.maximum(values, -bound), bound).astype(kind)


def setup_inputs(seed: int = 0) -> dict:
    splits = jax.random.split(jax.random.key(seed), 8)
    inputs = normal_values(splits[0], (TOKENS, D), 1.0, 6.0, ((0, 128),))
    upstream = normal_values(splits[1], (TOKENS, D), 4.0, 24.0, ((0, 128),))
    experts = choose_distinct(splits[2], TOKENS, EXPERTS, TOP, 512)
    gate_probs = jnp.clip(jnp.exp(math.log(0.5) - 2.3025851 * jax.random.uniform(splits[3], (TOKENS, TOP), jnp.float32) ** block_levels(splits[3], (TOKENS, TOP), ((0, 128),), -0.2, 0.2)), 0.05, 0.5)
    gate_weight = normal_values(splits[4], (WINDOW, D, FF), D ** -0.5, 0.09375, ((0, 8), (2, 4)))
    up_weight = normal_values(splits[5], (WINDOW, D, FF), D ** -0.5, 0.09375, ((0, 8), (2, 4)))
    down_weight = normal_values(splits[6], (WINDOW, FF, D), FF ** -0.5, 0.15625, ((0, 8), (1, 4)))
    return dict(inputs=inputs, upstream=upstream, experts=experts, gate_probs=gate_probs, gate_weight=gate_weight, up_weight=up_weight, down_weight=down_weight)


def round_bf(value):
    return lax.optimization_barrier(value.astype(jnp.bfloat16)).astype(jnp.float32)


def slot_tables(expert_rows, prob_rows, window, capacity):
    tok_rows = expert_rows.shape[0]
    expert_ids = jnp.arange(window, dtype=jnp.int32)
    chosen = expert_rows[:, :, None] == expert_ids[None, None, :]
    member = jnp.any(chosen, axis=1)
    weight = jnp.sum(jnp.where(chosen, prob_rows[:, :, None], 0.0), axis=1)
    order_in = (jnp.cumsum(member.astype(jnp.int32), axis=0) - 1).astype(jnp.int32)
    slot_ids = jnp.arange(capacity, dtype=jnp.int32)
    onehot = member.T[:, None, :] & (order_in.T[:, None, :] == slot_ids[None, :, None])
    positions = jnp.arange(tok_rows, dtype=jnp.int32)
    source = jnp.sum(jnp.where(onehot, positions[None, None, :], 0), axis=2).astype(jnp.int32)
    filled = jnp.any(onehot, axis=2)
    slot_gate = jnp.sum(jnp.where(onehot, weight.T[:, None, :], 0.0), axis=2)
    return onehot, chosen, source, filled, slot_gate


def expert_backward(operands):
    rows, grads, scale, gate_w, up_w, down_w = operands
    count = rows.shape[0]
    part_width = FF // PIECES
    pre_gate = jnp.dot(rows, gate_w, preferred_element_type=jnp.float32)
    pre_up = jnp.dot(rows, up_w, preferred_element_type=jnp.float32)
    sigma = jax.nn.sigmoid(pre_gate)
    act = pre_gate * sigma
    hidden = act * pre_up
    back = jnp.dot(grads, down_w.T, preferred_element_type=jnp.float32)
    piece_prob = jnp.sum((hidden * back).reshape(count, PIECES, part_width), axis=2)
    slot_prob = jnp.sum(round_bf(piece_prob), axis=1).astype(jnp.bfloat16)
    scaled = scale.astype(jnp.float32)[:, None] * back
    grad_up_h = (scaled * act).astype(jnp.bfloat16)
    grad_gate_h = (scaled * pre_up * sigma * (1.0 + pre_gate * (1.0 - sigma))).astype(jnp.bfloat16)
    gate_pieces = gate_w.astype(jnp.float32).reshape(D, PIECES, part_width)
    up_pieces = up_w.astype(jnp.float32).reshape(D, PIECES, part_width)
    term_gate = jnp.einsum('rjf,djf->rjd', grad_gate_h.astype(jnp.float32).reshape(count, PIECES, part_width), gate_pieces)
    term_up = jnp.einsum('rjf,djf->rjd', grad_up_h.astype(jnp.float32).reshape(count, PIECES, part_width), up_pieces)
    slot_dx = jnp.sum(round_bf(term_gate + term_up), axis=1).astype(jnp.bfloat16)
    dy_scaled = (scale.astype(jnp.float32)[:, None] * grads.astype(jnp.float32)).astype(jnp.bfloat16)
    hidden_b = hidden.astype(jnp.bfloat16)
    per_group = BLOCKS // GROUPS
    rows_g = rows.astype(jnp.float32).reshape(per_group, GROUPS, CAP, D)
    scaled_g = dy_scaled.astype(jnp.float32).reshape(per_group, GROUPS, CAP, D)
    gate_g = grad_gate_h.astype(jnp.float32).reshape(per_group, GROUPS, CAP, FF)
    up_g = grad_up_h.astype(jnp.float32).reshape(per_group, GROUPS, CAP, FF)
    hidden_g = hidden_b.astype(jnp.float32).reshape(per_group, GROUPS, CAP, FF)
    part_gate = jnp.einsum('mcrd,mcrf->cdf', rows_g, gate_g)
    part_up = jnp.einsum('mcrd,mcrf->cdf', rows_g, up_g)
    part_down = jnp.einsum('mcrf,mcrd->cfd', hidden_g, scaled_g)
    grad_gate = jnp.sum(round_bf(part_gate), axis=0).astype(jnp.bfloat16)
    grad_up = jnp.sum(round_bf(part_up), axis=0).astype(jnp.bfloat16)
    grad_down = jnp.sum(round_bf(part_down), axis=0).astype(jnp.bfloat16)
    return slot_dx, slot_prob, grad_gate, grad_up, grad_down


def combine_block(operands):
    onehot, chosen, dx_slots, prob_slots = operands
    summed = jnp.einsum('est,esd->td', onehot.astype(jnp.float32), dx_slots.astype(jnp.float32))
    per_expert = jnp.sum(jnp.where(onehot, prob_slots.astype(jnp.float32)[:, :, None], 0.0), axis=1)
    probs = jnp.sum(jnp.where(chosen, per_expert.T[:, None, :], 0.0), axis=2)
    return summed.astype(jnp.bfloat16), probs.astype(jnp.float32)


def reference(inputs, upstream, experts, gate_probs, gate_weight, up_weight, down_weight):
    input_blocks = inputs.reshape(BLOCKS, TOK_DEV, D)
    grad_blocks = upstream.reshape(BLOCKS, TOK_DEV, D)
    tables = jax.vmap(lambda rows_e, rows_p: slot_tables(rows_e, rows_p, WINDOW, CAP))(
        experts.reshape(BLOCKS, TOK_DEV, TOP), gate_probs.reshape(BLOCKS, TOK_DEV, TOP))
    onehot, chosen, source, filled, slot_gate = tables

    def pick_rows(block, where_from, usable):
        taken = jnp.take(block, where_from.reshape(-1), axis=0).reshape(WINDOW, CAP, D)
        return taken * usable[..., None].astype(jnp.bfloat16)

    row_slots = jax.vmap(pick_rows)(input_blocks, source, filled)
    grad_slots = jax.vmap(pick_rows)(grad_blocks, source, filled)
    gate_slots = slot_gate.astype(jnp.bfloat16)
    by_expert = (
        jnp.transpose(row_slots, (1, 0, 2, 3)).reshape(WINDOW, BLOCKS * CAP, D),
        jnp.transpose(grad_slots, (1, 0, 2, 3)).reshape(WINDOW, BLOCKS * CAP, D),
        jnp.transpose(gate_slots, (1, 0, 2)).reshape(WINDOW, BLOCKS * CAP),
        gate_weight, up_weight, down_weight)
    slot_dx, slot_prob, grad_gate, grad_up, grad_down = lax.map(expert_backward, by_expert)
    dx_blocks = jnp.transpose(slot_dx.reshape(WINDOW, BLOCKS, CAP, D), (1, 0, 2, 3))
    prob_blocks = jnp.transpose(slot_prob.reshape(WINDOW, BLOCKS, CAP), (1, 0, 2))
    grad_inputs, grad_probs = lax.map(combine_block, (onehot, chosen, dx_blocks, prob_blocks))
    return (grad_inputs.reshape(TOKENS, D), grad_probs.reshape(TOKENS, TOP), grad_gate, grad_up, grad_down)
```

```python
import functools

import jax
import jax.numpy as jnp
from jax import lax
from jax.experimental import pallas as pl
from jax.experimental.pallas import tpu as pltpu
from jax.sharding import PartitionSpec as P

CAP = 24
F32 = jnp.float32
BF = jnp.bfloat16


def slot_tables(expert_rows, prob_rows, expert_ids, capacity):
    tok_rows = expert_rows.shape[0]
    chosen = expert_rows[:, :, None] == expert_ids[None, None, :]
    member = jnp.any(chosen, axis=1)
    weight = jnp.sum(jnp.where(chosen, prob_rows[:, :, None], 0.0), axis=1)
    order_in = jnp.cumsum(member.astype(jnp.int32), axis=0) - 1
    slot_ids = jnp.arange(capacity, dtype=jnp.int32)
    onehot = member.T[:, None, :] & (order_in.T[:, None, :] == slot_ids[None, :, None])
    slot_gate = jnp.sum(jnp.where(onehot, weight.T[:, None, :], 0.0), axis=2)
    return onehot, chosen, slot_gate


def pick_kernel(onehot_ref, gate_ref, x_ref, dy_ref, out_ref):
    step = pl.program_id(0)
    half = pl.num_programs(0) // 2

    @pl.when(step < half)
    def _():
        out_ref[...] = jnp.dot(onehot_ref[...], x_ref[...], preferred_element_type=F32).astype(BF)

    @pl.when(step >= half)
    def _():
        rows = jnp.dot(onehot_ref[...], dy_ref[...], preferred_element_type=F32)
        out_ref[...] = (rows * gate_ref[...]).astype(BF)


def pick_rows(onehot, gate, inputs, upstream):
    slots, tokens = onehot.shape
    width = inputs.shape[1]
    block = 1024
    half = width // block
    return pl.pallas_call(
        pick_kernel,
        grid=(2 * half,),
        in_specs=[
            pl.BlockSpec((slots, tokens), lambda i: (0, 0)),
            pl.BlockSpec((slots, 1), lambda i: (0, 0)),
            pl.BlockSpec((tokens, block), lambda i: (0, jnp.minimum(i, half - 1))),
            pl.BlockSpec((tokens, block), lambda i: (0, jnp.maximum(i - half, 0))),
        ],
        out_specs=pl.BlockSpec((slots, block), lambda i: (0, i)),
        out_shape=jax.ShapeDtypeStruct((slots, 2 * width), BF),
        compiler_params=pltpu.CompilerParams(vmem_limit_bytes=32 * 2**20),
        cost_estimate=pl.CostEstimate(
            flops=4 * slots * tokens * width, bytes_accessed=8 * tokens * width, transcendentals=0
        ),
    )(onehot, gate, inputs, upstream)


def ring(axis):
    size = lax.axis_size(axis)
    to_right = [(i, (i + 1) % size) for i in range(size)]
    to_left = [(i, (i - 1) % size) for i in range(size)]
    return to_right, to_left


def ring_gather(block, axis):
    to_right, to_left = ring(axis)
    half = block.shape[0] // 2
    left = lax.ppermute(block, axis, to_right)
    right = lax.ppermute(block, axis, to_left)
    far_a = lax.ppermute(left[:half], axis, to_right)
    far_b = lax.ppermute(right[half:], axis, to_left)
    return [block, left, right, far_a, far_b]


def add_bf(a, b):
    return (a.astype(F32) + b.astype(F32)).astype(BF)


def ring_sum(own, left, right, far, axis):
    to_right, to_left = ring(axis)
    half = own.shape[0] // 2
    got_a = lax.ppermute(far[:half], axis, to_right)
    got_b = lax.ppermute(far[half:], axis, to_left)
    right = jnp.concatenate([add_bf(right[:half], got_a), right[half:]])
    left = jnp.concatenate([left[:half], add_bf(left[half:], got_b)])
    from_left = lax.ppermute(right, axis, to_right)
    from_right = lax.ppermute(left, axis, to_left)
    return own.astype(F32) + from_left.astype(F32) + from_right.astype(F32)


def body(inputs, upstream, experts, gate_probs, gate_weight, up_weight, down_weight):
    experts_n = lax.axis_size("ep")
    layers = experts_n // 2
    width = inputs.shape[1]
    me = lax.axis_index("ep")
    z, core = me // 2, me % 2
    far_order = [(dc, dz) for dc in range(2) for dz in range(layers)]
    expert_ids = jnp.stack([2 * ((z + dz) % layers) + (core ^ dc) for dc, dz in far_order]).astype(jnp.int32)
    swap = [(2 * i + j, 2 * i + 1 - j) for i in range(layers) for j in range(2)]

    def shift(dz):
        return [(2 * i + j, 2 * ((i + dz) % layers) + j) for i in range(layers) for j in range(2)]

    onehot, chosen, slot_gate = slot_tables(experts, gate_probs, expert_ids, CAP)
    slots = experts_n * CAP
    pick = onehot.astype(BF).reshape(slots, -1)
    gate = slot_gate.astype(BF).astype(F32).reshape(slots, 1)
    sent = pick_rows(pick, gate, inputs, upstream).reshape(2, layers, CAP, 2 * width)
    other = lax.ppermute(sent[1], "ep", swap)

    gate_w, up_w, down_w = gate_weight[0], up_weight[0], down_weight[0]
    order = [0, 1, 3, 2]
    chunks, grads_g, grads_u, hiddens, probs = {}, {}, {}, {}, {}
    for dz in order:
        block = jnp.concatenate([sent[0, dz], other[dz]])
        if dz:
            block = lax.ppermute(block, "ep", shift(dz))
        both = jnp.concatenate(ring_gather(block, "etp"))
        rows, grads = both[:, :width], both[:, width:]
        pre_gate = jnp.dot(rows, gate_w, preferred_element_type=F32)
        pre_up = jnp.dot(rows, up_w, preferred_element_type=F32)
        back = lax.dot_general(grads, down_w, (((1,), (1,)), ((), ())), preferred_element_type=F32)
        sigma = jax.nn.sigmoid(pre_gate)
        act = pre_gate * sigma
        hidden = act * pre_up
        chunks[dz] = both
        probs[dz] = jnp.sum(hidden * back, axis=1, keepdims=True).astype(BF)
        hiddens[dz] = hidden.astype(BF)
        grads_u[dz] = (back * act).astype(BF)
        grads_g[dz] = (back * pre_up * sigma * (1.0 + pre_gate * (1.0 - sigma))).astype(BF)

    every = jnp.concatenate([chunks[dz] for dz in order])
    grad_g = jnp.concatenate([grads_g[dz] for dz in order])
    grad_u = jnp.concatenate([grads_u[dz] for dz in order])
    hidden_b = jnp.concatenate([hiddens[dz] for dz in order])
    both_g = jnp.concatenate([grad_g, grad_u], axis=1)
    part = gate_w.shape[1]

    groups = lax.axis_size("dp")
    slice_w = width // groups
    mine = lax.axis_index("dp")

    def weight_block(ahead):
        at = ((mine + ahead) % groups) * slice_w
        rows = lax.dynamic_slice(every, (0, at), (every.shape[0], slice_w))
        grads = lax.dynamic_slice(every, (0, at + width), (every.shape[0], slice_w))
        over_rows = (((0,), (0,)), ((), ()))
        top = lax.dot_general(both_g, rows, over_rows, preferred_element_type=F32).astype(BF)
        low = lax.dot_general(hidden_b, grads, over_rows, preferred_element_type=F32).astype(BF)
        return jnp.concatenate([top, low])

    far_w, right_w, left_w, own_w = (weight_block(k) for k in (2, 1, groups - 1, 0))
    summed = ring_sum(own_w, left_w, right_w, far_w, "dp")

    returned = {}
    by_f = (((1,), (1,)), ((), ()))
    for dz in reversed(order):
        dx = lax.dot_general(grads_g[dz], gate_w, by_f, preferred_element_type=F32)
        dx = dx + lax.dot_general(grads_u[dz], up_w, by_f, preferred_element_type=F32)
        dx = jnp.concatenate([dx.astype(BF), jnp.broadcast_to(probs[dz], (dx.shape[0], 128))], axis=1)
        own, left, right, far = (dx[i * 2 * CAP : (i + 1) * 2 * CAP] for i in range(4))
        block = ring_sum(own, left, right, far, "etp").astype(BF)
        if dz:
            block = lax.ppermute(block, "ep", shift(layers - dz))
        returned[dz] = block
    mine_rows = jnp.stack([returned[dz][:CAP] for dz in range(layers)])
    others = lax.ppermute(jnp.stack([returned[dz][CAP:] for dz in range(layers)]), "ep", swap)
    dx_slots = jnp.concatenate([mine_rows, others]).reshape(slots, width + 128)
    grad_inputs = lax.dot_general(
        pick, dx_slots[:, :width], (((0,), (0,)), ((), ())), preferred_element_type=F32
    ).astype(BF)
    prob_sum = dx_slots[:, width].astype(F32).reshape(experts_n, CAP)
    gates = gate.reshape(experts_n, CAP)
    prob_slots = (prob_sum / jnp.where(gates > 0, gates, 1.0)).astype(BF).astype(F32)
    per_expert = jnp.sum(jnp.where(onehot, prob_slots[:, :, None], 0.0), axis=1)
    grad_probs = jnp.sum(jnp.where(chosen, per_expert.T[:, None, :], 0.0), axis=2)

    grad_gate = summed[:part].T.astype(BF)[None]
    grad_up = summed[part : 2 * part].T.astype(BF)[None]
    grad_down = summed[2 * part :].astype(BF)[None]
    return (grad_inputs, grad_probs, grad_gate, grad_up, grad_down)


def solution(mesh):
    tokens = P(("ep", "etp", "dp"), None)
    return jax.shard_map(
        body,
        mesh=mesh,
        in_specs=(tokens, tokens, tokens, tokens, P("ep", None, "etp"), P("ep", None, "etp"), P("ep", "etp", None)),
        out_specs=(tokens, tokens, P("ep", "dp", "etp"), P("ep", "dp", "etp"), P("ep", "etp", "dp")),
        check_vma=False,
    )
```

```python
import functools

import jax
import jax.numpy as jnp
from jax import lax
from jax.experimental import pallas as pl
from jax.experimental.pallas import tpu as pltpu
from jax.sharding import PartitionSpec as P

CAP = 24
LANES = 128
F32 = jnp.float32
BF = jnp.bfloat16
MIB = 2**20
BY_LAST = (((1,), (1,)), ((), ()))
BY_FIRST = (((0,), (0,)), ((), ()))


def dot(a, b):
    return jnp.dot(a, b, preferred_element_type=F32)


def cost(flops, size):
    return pl.CostEstimate(flops=int(flops), bytes_accessed=int(size), transcendentals=0)


def limit(mib):
    return pltpu.CompilerParams(vmem_limit_bytes=mib * MIB)


def slot_tables(expert_rows, prob_rows, expert_ids, capacity):
    tok_rows = expert_rows.shape[0]
    chosen = expert_rows[:, :, None] == expert_ids[None, None, :]
    member = jnp.any(chosen, axis=1)
    weight = jnp.sum(jnp.where(chosen, prob_rows[:, :, None], 0.0), axis=1)
    order_in = jnp.cumsum(member.astype(jnp.int32), axis=0) - 1
    slot_ids = jnp.arange(capacity, dtype=jnp.int32)
    onehot = member.T[:, None, :] & (order_in.T[:, None, :] == slot_ids[None, :, None])
    slot_gate = jnp.sum(jnp.where(onehot, weight.T[:, None, :], 0.0), axis=2)
    return onehot, chosen, slot_gate


def pick_kernel(onehot_ref, gate_ref, x_ref, dy_ref, own_ref, other_ref):
    step = pl.program_id(0)
    half = pl.num_programs(0) // 2
    mid = own_ref.shape[0]

    @pl.when(step < half)
    def _():
        rows = dot(onehot_ref[...], x_ref[...]).astype(BF)
        own_ref[...] = rows[:mid]
        other_ref[...] = rows[mid:]

    @pl.when(step >= half)
    def _():
        rows = (dot(onehot_ref[...], dy_ref[...]) * gate_ref[...]).astype(BF)
        own_ref[...] = rows[:mid]
        other_ref[...] = rows[mid:]


def pick_rows(onehot, gate, inputs, upstream):
    slots, tokens = onehot.shape
    width = inputs.shape[1]
    block = 1024
    half = width // block
    out = jax.ShapeDtypeStruct((slots // 2, 2 * width), BF)
    spec = pl.BlockSpec((slots // 2, block), lambda i: (0, i))
    return pl.pallas_call(
        pick_kernel,
        grid=(2 * half,),
        in_specs=[
            pl.BlockSpec((slots, tokens), lambda i: (0, 0)),
            pl.BlockSpec((slots, 1), lambda i: (0, 0)),
            pl.BlockSpec((tokens, block), lambda i: (0, jnp.minimum(i, half - 1))),
            pl.BlockSpec((tokens, block), lambda i: (0, jnp.maximum(i - half, 0))),
        ],
        out_specs=[spec, spec],
        out_shape=[out, out],
        compiler_params=limit(12),
        cost_estimate=cost(4 * slots * tokens * width, 8 * tokens * width),
    )(onehot, gate, inputs, upstream)


def forward_kernel(*refs):
    x_parts, dy_parts = refs[:5], refs[5:10]
    gate_ref, up_ref, down_ref = refs[10:13]
    x_ref, dy_ref, grads_ref, grads_t_ref, hidden_t_ref, prob_ref = refs[-9:-3]
    acc_g, acc_u, acc_b = refs[-3:]
    step = pl.program_id(0)

    @pl.when(step == 0)
    def _():
        acc_g[...] = jnp.zeros_like(acc_g)
        acc_u[...] = jnp.zeros_like(acc_u)
        acc_b[...] = jnp.zeros_like(acc_b)

    at = 0
    for x_part, dy_part in zip(x_parts, dy_parts):
        rows = x_part.shape[0]
        x_ref[at : at + rows, :] = x_part[...]
        dy_ref[at : at + rows, :] = dy_part[...]
        at += rows
    x = x_ref[...]
    acc_g[...] += dot(x, gate_ref[...])
    acc_u[...] += dot(x, up_ref[...])
    acc_b[...] += lax.dot_general(dy_ref[...], down_ref[...], BY_LAST, preferred_element_type=F32)

    @pl.when(step == pl.num_programs(0) - 1)
    def _():
        pre_gate, pre_up, back = acc_g[...], acc_u[...], acc_b[...]
        part = pre_gate.shape[1]
        sigma = jax.nn.sigmoid(pre_gate)
        act = pre_gate * sigma
        hidden = act * pre_up
        prob = jnp.sum(hidden * back, axis=1, keepdims=True)
        prob_ref[...] = jnp.broadcast_to(prob, prob_ref.shape).astype(BF)
        grad_g = back * pre_up * sigma * (1.0 + pre_gate * (1.0 - sigma))
        grad_u = back * act
        grads_ref[:, :part] = grad_g.astype(BF)
        grads_ref[:, part:] = grad_u.astype(BF)
        grads_t_ref[:part, :] = grad_g.T.astype(BF)
        grads_t_ref[part:, :] = grad_u.T.astype(BF)
        hidden_t_ref[...] = hidden.T.astype(BF)


def forward(parts, gate_w, up_w, down_w, after):
    width, part = gate_w.shape
    count = sum(p.shape[0] for p in parts)
    block = 1024
    steps = width // block
    return pl.pallas_call(
        forward_kernel,
        grid=(steps,),
        in_specs=[pl.BlockSpec((p.shape[0], block), lambda i: (0, i)) for p in parts]
        + [pl.BlockSpec((p.shape[0], block), lambda i: (0, i + steps)) for p in parts]
        + [
            pl.BlockSpec((block, part), lambda i: (i, 0)),
            pl.BlockSpec((block, part), lambda i: (i, 0)),
            pl.BlockSpec((part, block), lambda i: (0, i)),
        ]
        + [pl.BlockSpec(memory_space=pl.ANY)] * len(after),
        out_specs=[
            pl.BlockSpec((count, block), lambda i: (0, i)),
            pl.BlockSpec((count, block), lambda i: (0, i)),
            pl.BlockSpec((count, 2 * part), lambda i: (0, 0)),
            pl.BlockSpec((2 * part, count), lambda i: (0, 0)),
            pl.BlockSpec((part, count), lambda i: (0, 0)),
            pl.BlockSpec((count, LANES), lambda i: (0, 0)),
        ],
        out_shape=[
            jax.ShapeDtypeStruct((count, width), BF),
            jax.ShapeDtypeStruct((count, width), BF),
            jax.ShapeDtypeStruct((count, 2 * part), BF),
            jax.ShapeDtypeStruct((2 * part, count), BF),
            jax.ShapeDtypeStruct((part, count), BF),
            jax.ShapeDtypeStruct((count, LANES), BF),
        ],
        scratch_shapes=[pltpu.VMEM((count, part), F32)] * 3,
        compiler_params=limit(30),
        cost_estimate=cost(6 * count * width * part, 6 * width * part + 8 * count * width),
    )(*parts, *parts, gate_w, up_w, down_w, *after)


def weight_kernel(groups, outs, at_ref, *refs):
    x_refs, dy_refs = refs[:groups], refs[groups : 2 * groups]
    g_refs, h_refs = refs[2 * groups : 3 * groups], refs[3 * groups : 4 * groups]
    out_refs = refs[-outs:]
    top = sum(dot(g[...], x[...]) for g, x in zip(g_refs, x_refs)).astype(BF)
    low = sum(dot(h[...], d[...]) for h, d in zip(h_refs, dy_refs)).astype(BF)
    if outs == 1:
        out_refs[0][0, : top.shape[0], :] = top
        out_refs[0][0, top.shape[0] :, :] = low
    else:
        half = out_refs[0].shape[1]
        out_refs[0][0] = top[:half]
        out_refs[1][0, : top.shape[0] - half, :] = top[half:]
        out_refs[1][0, top.shape[0] - half :, :] = low


def weight_blocks(at, slice_w, xs, dys, grads_t, hiddens_t, outs, after=()):
    block = 512
    steps = slice_w // block
    count = at.shape[0]
    rows = grads_t[0].shape[0] + hiddens_t[0].shape[0]
    tall = [pl.BlockSpec((v.shape[0], block), lambda k, i, at: (0, at[k] * steps + i)) for v in xs]
    whole = [pl.BlockSpec(v.shape, lambda k, i, at: (0, 0)) for v in list(grads_t) + list(hiddens_t)]
    spec = pl.BlockSpec((1, rows // outs, block), lambda k, i, at: (k, 0, i))
    return pl.pallas_call(
        functools.partial(weight_kernel, len(xs), outs),
        grid_spec=pltpu.PrefetchScalarGridSpec(
            num_scalar_prefetch=1,
            grid=(count, steps),
            in_specs=tall + tall + whole + [pl.BlockSpec(memory_space=pl.ANY)] * len(after),
            out_specs=[spec] * outs,
        ),
        out_shape=[jax.ShapeDtypeStruct((count, rows // outs, slice_w), BF)] * outs,
        compiler_params=limit(20),
        cost_estimate=cost(count * 2 * rows * slice_w * sum(v.shape[0] for v in xs), count * 7 * MIB),
    )(at, *xs, *dys, *grads_t, *hiddens_t, *after)


def join_kernel(a_ref, b_ref, *refs):
    out_ref = refs[-1]
    rows = a_ref.shape[0]
    out_ref[:rows, :] = a_ref[...]
    out_ref[rows:, :] = b_ref[...]


def join_rows(a, b, after):
    block = 2048
    spec = pl.BlockSpec((a.shape[0], block), lambda i: (0, i))
    return pl.pallas_call(
        join_kernel,
        grid=(a.shape[1] // block,),
        in_specs=[spec, spec] + [pl.BlockSpec(memory_space=pl.ANY)] * len(after),
        out_specs=pl.BlockSpec((2 * a.shape[0], block), lambda i: (0, i)),
        out_shape=jax.ShapeDtypeStruct((2 * a.shape[0], a.shape[1]), BF),
        compiler_params=limit(8),
        cost_estimate=cost(0, 8 * a.size),
    )(a, b, *after)


def pass_kernel(*refs):
    pass


def order(value, after):
    spec = pl.BlockSpec(memory_space=pl.ANY)
    return pl.pallas_call(
        pass_kernel,
        in_specs=[spec] * (1 + len(after)),
        out_specs=spec,
        out_shape=jax.ShapeDtypeStruct(value.shape, value.dtype),
        input_output_aliases={0: 0},
        cost_estimate=cost(0, 0),
    )(value, *after)


def add_rows(a, b):
    return (a.astype(F32) + b.astype(F32)).astype(BF)


def dp_add_kernel(rest_ref, far_a_ref, far_b_ref, right_ref, left_ref):
    half = far_a_ref.shape[0]
    right_ref[:half, :] = add_rows(rest_ref[0, :half], far_a_ref[...])
    right_ref[half:, :] = rest_ref[0, half:]
    left_ref[:half, :] = rest_ref[1, :half]
    left_ref[half:, :] = add_rows(rest_ref[1, half:], far_b_ref[...])


def dp_add(rest, far_a, far_b):
    _, rows, width = rest.shape
    block = 256
    spec = pl.BlockSpec((rows // 2, block), lambda i: (0, i))
    out = pl.BlockSpec((rows, block), lambda i: (0, i))
    return pl.pallas_call(
        dp_add_kernel,
        grid=(width // block,),
        in_specs=[pl.BlockSpec((2, rows, block), lambda i: (0, 0, i)), spec, spec],
        out_specs=[out, out],
        out_shape=[jax.ShapeDtypeStruct((rows, width), BF)] * 2,
        compiler_params=limit(12),
        cost_estimate=cost(2 * rows * width, 10 * rows * width),
    )(rest, far_a, far_b)


def etp_add_kernel(left_ref, right_ref, far_a_ref, far_b_ref, *refs):
    left_out, right_out = refs[-2:]
    cut = far_a_ref.shape[0]
    right_out[:cut, :] = add_rows(right_ref[:cut], far_a_ref[...])
    right_out[cut:, :] = right_ref[cut:]
    left_out[:cut, :] = left_ref[:cut]
    left_out[cut:, :] = add_rows(left_ref[cut:], far_b_ref[...])


def etp_add(left, right, far_a, far_b, after):
    rows, width = left.shape
    block = 11 * LANES
    parts = (left, right, far_a, far_b)
    spec = pl.BlockSpec((rows, block), lambda i: (0, i))
    return pl.pallas_call(
        etp_add_kernel,
        grid=(width // block,),
        in_specs=[pl.BlockSpec((p.shape[0], block), lambda i: (0, i)) for p in parts]
        + [pl.BlockSpec(memory_space=pl.ANY)] * len(after),
        out_specs=[spec, spec],
        out_shape=[jax.ShapeDtypeStruct((rows, width), BF)] * 2,
        compiler_params=limit(12),
        cost_estimate=cost(rows * width, 10 * rows * width),
    )(*parts, *after)


def dx_kernel(sources, bands, *refs):
    grads, probs = refs[:sources], refs[sources : 2 * sources]
    gate_ref, up_ref = refs[2 * sources : 2 * sources + 2]
    out_refs, lhs, sums = refs[-len(bands) - 2 : -2], refs[-2], refs[-1]

    @pl.when(pl.program_id(0) == 0)
    def _():
        at = 0
        for grad, prob in zip(grads, probs):
            rows = grad.shape[0]
            lhs[at : at + rows, :] = grad[...]
            sums[at : at + rows, :] = prob[...]
            at += rows

    part = gate_ref.shape[1]
    total = lax.dot_general(lhs[:, :part], gate_ref[...], BY_LAST, preferred_element_type=F32)
    total += lax.dot_general(lhs[:, part:], up_ref[...], BY_LAST, preferred_element_type=F32)
    total = total.astype(BF)
    for out, band in zip(out_refs, bands):
        to = 0
        for at, rows in band:
            out[to : to + rows, :] = total[at : at + rows]
            to += rows

    @pl.when(pl.program_id(0) == pl.num_programs(0) - 1)
    def _():
        for out, band in zip(out_refs, bands):
            to = 0
            for at, rows in band:
                out[to : to + rows, out.shape[1] - LANES :] = sums[at : at + rows, :]
                to += rows


def dx_blocks(grads, probs, gate_w, up_w, bands, after):
    width, part = gate_w.shape
    count = sum(g.shape[0] for g in grads)
    block = 11 * LANES
    steps = (width + LANES) // block
    sizes = [sum(rows for _, rows in band) for band in bands]
    return pl.pallas_call(
        functools.partial(dx_kernel, len(grads), bands),
        grid=(steps,),
        in_specs=[pl.BlockSpec(v.shape, lambda i: (0, 0)) for v in (*grads, *probs)]
        + [pl.BlockSpec((block, part), lambda i: (i, 0))] * 2
        + [pl.BlockSpec(memory_space=pl.ANY)] * len(after),
        out_specs=[pl.BlockSpec((rows, block), lambda i: (0, i)) for rows in sizes],
        out_shape=[jax.ShapeDtypeStruct((rows, width + LANES), BF) for rows in sizes],
        scratch_shapes=[pltpu.VMEM((count, 2 * part), BF), pltpu.VMEM((count, LANES), BF)],
        compiler_params=limit(30),
        cost_estimate=cost(4 * count * width * part, 4 * width * part + 2 * count * width),
    )(*grads, *probs, gate_w, up_w, *after)


def final_kernel(own_ref, left_ref, right_ref, gate_ref, up_ref, down_ref):
    total = own_ref[0].astype(F32) + left_ref[...].astype(F32) + right_ref[...].astype(F32)
    part = down_ref.shape[0]
    gate_ref[...] = total[:part].T.astype(BF)
    up_ref[...] = total[part : 2 * part].T.astype(BF)
    down_ref[...] = total[2 * part :].astype(BF)


def final_sum(rest, left, right):
    rows, width = left.shape
    part = rows // 3
    block = 256
    spec = pl.BlockSpec((rows, block), lambda i: (0, i))
    tall = pl.BlockSpec((block, part), lambda i: (i, 0))
    return pl.pallas_call(
        final_kernel,
        grid=(width // block,),
        in_specs=[pl.BlockSpec((1, rows, block), lambda i: (2, 0, i)), spec, spec],
        out_specs=[tall, tall, pl.BlockSpec((part, block), lambda i: (0, i))],
        out_shape=[jax.ShapeDtypeStruct((width, part), BF)] * 2 + [jax.ShapeDtypeStruct((part, width), BF)],
        compiler_params=limit(16),
        cost_estimate=cost(rows * width, 8 * rows * width),
    )(rest, left, right)


def split_band(band, size):
    first, second = [], []
    for at, rows in band:
        take = min(rows, size)
        if take:
            first.append((at, take))
        if rows > take:
            second.append((at + take, rows - take))
        size -= take
    return [first, second]


def ring(axis):
    size = lax.axis_size(axis)
    return [(i, (i + 1) % size) for i in range(size)], [(i, (i - 1) % size) for i in range(size)]


def ring_gather(block, axis, cut, after=()):
    to_right, to_left = ring(axis)
    left = lax.ppermute(block, axis, to_right)
    right = lax.ppermute(block, axis, to_left)
    if after:
        left, right = order(left, after), order(right, after)
    far_a = lax.ppermute(left[:cut], axis, to_right)
    far_b = lax.ppermute(right[cut:], axis, to_left)
    return [block, left, right, far_a, far_b]


def ring_first(far_a, far_b, axis):
    to_right, to_left = ring(axis)
    return lax.ppermute(far_a, axis, to_right), lax.ppermute(far_b, axis, to_left)


def ring_second(left, right, axis):
    to_right, to_left = ring(axis)
    return lax.ppermute(right, axis, to_right), lax.ppermute(left, axis, to_left)


def body(inputs, upstream, experts, gate_probs, gate_weight, up_weight, down_weight):
    experts_n = lax.axis_size("ep")
    layers = experts_n // 2
    width = inputs.shape[1]
    me = lax.axis_index("ep")
    z, core = me // 2, me % 2
    expert_ids = jnp.stack(
        [2 * ((z + dz) % layers) + (core ^ dc) for dc in range(2) for dz in range(layers)]
    ).astype(jnp.int32)
    swap = [(2 * i + j, 2 * i + 1 - j) for i in range(layers) for j in range(2)]

    def shift(dz):
        return [(2 * i + j, 2 * ((i + dz) % layers) + j) for i in range(layers) for j in range(2)]

    onehot, chosen, slot_gate = slot_tables(experts, gate_probs, expert_ids, CAP)
    slots = experts_n * CAP
    pick = onehot.astype(BF).reshape(slots, -1)
    gate = slot_gate.astype(BF).astype(F32).reshape(slots, 1)
    mine, others = pick_rows(pick, gate, inputs, upstream)
    others = lax.ppermute(others, "ep", swap)

    gate_w, up_w, down_w = gate_weight[0], up_weight[0], down_weight[0]
    blocks = {}
    for dz in range(layers):
        at = slice(dz * CAP, (dz + 1) * CAP)
        block = jnp.concatenate([mine[at], others[at]])
        if dz == 2:
            block = order(block, (blocks[1],))
        blocks[dz] = lax.ppermute(block, "ep", shift(dz)) if dz else block
    groups = [(0,), (1, 3), (2,)]
    cuts = [32, 48, 16]
    xs, dys, grads, grads_t, hiddens_t, probs = [], [], [], [], [], []
    parts = [None] * len(groups)
    for i, (group, cut) in enumerate(zip(groups, cuts)):
        after = ()
        if i == 1:
            block = join_rows(blocks[group[0]], blocks[group[1]], tuple(parts[0][1:3]))
        elif i == 2:
            block = order(blocks[group[0]], tuple(parts[1][1:3] + parts[0][3:]))
            after = (probs[0], *parts[1][3:])
        else:
            block = blocks[group[0]]
        parts[i] = ring_gather(block, "etp", cut, after)
        results = forward(parts[i], gate_w, up_w, down_w, probs[-1:])
        for kept, result in zip((xs, dys, grads, grads_t, hiddens_t, probs), results):
            kept.append(result)

    dp = lax.axis_size("dp")
    slice_w = width // dp
    my_dp = lax.axis_index("dp")

    def weights_for(ahead, outs, after=()):
        at = jnp.stack([(my_dp + k) % dp for k in ahead]).astype(jnp.int32)
        return weight_blocks(at, slice_w, xs, dys, grads_t, hiddens_t, outs, after)

    far_a, far_b = weights_for((2,), 2)
    got_wa, got_wb = ring_first(far_a[0], far_b[0], "dp")

    step = 2 * CAP
    plans = [
        ((1, 2), (1, 3, 2), [(0, 2 * step), (8 * step, step)], 80, 64),
        ((0,), (0,), [(0, step)], 16, 32),
    ]
    pieces, got = [], []
    after = (far_a,)
    for sources, members, firsts, size_a, size_b in plans:
        bands = [[(at + k * rows, rows) for at, rows in firsts] for k in range(3)]
        far = [(at + 3 * rows, rows) for at, rows in firsts]
        bands += split_band(far, size_a)
        out = dx_blocks([grads[k] for k in sources], [probs[k] for k in sources], gate_w, up_w, bands, after)
        pieces.append(out)
        got.append(ring_first(out[3], out[4], "etp"))
        after = (out[0],)

    (rest,) = weights_for((1, dp - 1, 0), 1, after)
    right_w, left_w = dp_add(rest, got_wa, got_wb)
    from_left_w, from_right_w = ring_second(left_w, right_w, "dp")

    returned = {}
    for (sources, members, *_), out, far in zip(plans, pieces, got):
        own, left, right = out[:3]
        left, right = etp_add(left, right, *far, (right_w,))
        from_left, from_right = ring_second(left, right, "etp")
        total = (own.astype(F32) + from_left.astype(F32) + from_right.astype(F32)).astype(BF)
        for i, dz in enumerate(members):
            block = total[i * step : (i + 1) * step]
            returned[dz] = lax.ppermute(block, "ep", shift(layers - dz)) if dz else block
    mine_rows = jnp.concatenate([returned[dz][:CAP] for dz in range(layers)])
    others = jnp.concatenate([returned[dz][CAP:] for dz in range(layers)])
    others = lax.ppermute(others, "ep", swap)
    dx_slots = jnp.concatenate([mine_rows, others])
    grad_inputs = lax.dot_general(pick, dx_slots[:, :width], BY_FIRST, preferred_element_type=F32).astype(BF)
    prob_sum = dx_slots[:, width].astype(F32).reshape(experts_n, CAP)
    gates = gate.reshape(experts_n, CAP)
    prob_slots = (prob_sum / jnp.where(gates > 0, gates, 1.0)).astype(BF).astype(F32)
    per_expert = jnp.sum(jnp.where(onehot, prob_slots[:, :, None], 0.0), axis=1)
    grad_probs = jnp.sum(jnp.where(chosen, per_expert.T[:, None, :], 0.0), axis=2)

    grad_gate, grad_up, grad_down = final_sum(rest, from_left_w, from_right_w)
    return (grad_inputs, grad_probs, grad_gate[None], grad_up[None], grad_down[None])


def solution(mesh):
    tokens = P(("ep", "etp", "dp"), None)
    return jax.shard_map(
        body,
        mesh=mesh,
        in_specs=(tokens, tokens, tokens, tokens, P("ep", None, "etp"), P("ep", None, "etp"), P("ep", "etp", None)),
        out_specs=(tokens, tokens, P("ep", "dp", "etp"), P("ep", "dp", "etp"), P("ep", "etp", "dp")),
        check_vma=False,
    )
```

```python
import functools

import jax
import jax.numpy as jnp
from jax import lax
from jax.experimental import pallas as pl
from jax.experimental.pallas import tpu as pltpu
from jax.sharding import PartitionSpec as P

CAP = 24
LANES = 128
F32 = jnp.float32
BF = jnp.bfloat16
MIB = 2**20
BY_LAST = (((1,), (1,)), ((), ()))
BY_FIRST = (((0,), (0,)), ((), ()))


def dot(a, b):
    return jnp.dot(a, b, preferred_element_type=F32)


def cost(flops, size):
    return pl.CostEstimate(flops=int(flops), bytes_accessed=int(size), transcendentals=0)


def in_hbm(*values):
    return [pltpu.with_memory_space_constraint(v, pltpu.HBM) for v in values]


def limit(mib):
    return pltpu.CompilerParams(vmem_limit_bytes=mib * MIB)


def slot_tables(expert_rows, prob_rows, expert_ids, capacity):
    tok_rows = expert_rows.shape[0]
    chosen = expert_rows[:, :, None] == expert_ids[None, None, :]
    member = jnp.any(chosen, axis=1)
    weight = jnp.sum(jnp.where(chosen, prob_rows[:, :, None], 0.0), axis=1)
    order_in = jnp.cumsum(member.astype(jnp.int32), axis=0) - 1
    slot_ids = jnp.arange(capacity, dtype=jnp.int32)
    onehot = member.T[:, None, :] & (order_in.T[:, None, :] == slot_ids[None, :, None])
    slot_gate = jnp.sum(jnp.where(onehot, weight.T[:, None, :], 0.0), axis=2)
    return onehot, chosen, slot_gate


def pick_kernel(onehot_ref, gate_ref, x_ref, dy_ref, own_ref, other_ref):
    step = pl.program_id(0)
    half = pl.num_programs(0) // 2
    mid = own_ref.shape[0]

    @pl.when(step < half)
    def _():
        rows = dot(onehot_ref[...], x_ref[...]).astype(BF)
        own_ref[...] = rows[:mid]
        other_ref[...] = rows[mid:]

    @pl.when(step >= half)
    def _():
        rows = (dot(onehot_ref[...], dy_ref[...]) * gate_ref[...]).astype(BF)
        own_ref[...] = rows[:mid]
        other_ref[...] = rows[mid:]


def pick_rows(onehot, gate, inputs, upstream):
    slots, tokens = onehot.shape
    width = inputs.shape[1]
    block = 1024
    half = width // block
    out = jax.ShapeDtypeStruct((slots // 2, 2 * width), BF)
    spec = pl.BlockSpec((slots // 2, block), lambda i: (0, i))
    return pl.pallas_call(
        pick_kernel,
        grid=(2 * half,),
        in_specs=[
            pl.BlockSpec((slots, tokens), lambda i: (0, 0)),
            pl.BlockSpec((slots, 1), lambda i: (0, 0)),
            pl.BlockSpec((tokens, block), lambda i: (0, jnp.minimum(i, half - 1))),
            pl.BlockSpec((tokens, block), lambda i: (0, jnp.maximum(i - half, 0))),
        ],
        out_specs=[spec, spec],
        out_shape=[out, out],
        compiler_params=limit(12),
        cost_estimate=cost(4 * slots * tokens * width, 8 * tokens * width),
    )(onehot, gate, inputs, upstream)


def forward_kernel(parts, *refs):
    x_parts, dy_parts = refs[:parts], refs[parts : 2 * parts]
    gate_ref, up_ref, down_ref = refs[2 * parts : 2 * parts + 3]
    x_ref, dy_ref, grads_ref, grads_t_ref, hidden_t_ref, prob_ref = refs[-9:-3]
    acc_g, acc_u, acc_b = refs[-3:]
    step = pl.program_id(0)

    @pl.when(step == 0)
    def _():
        acc_g[...] = jnp.zeros_like(acc_g)
        acc_u[...] = jnp.zeros_like(acc_u)
        acc_b[...] = jnp.zeros_like(acc_b)

    at = 0
    for x_part, dy_part in zip(x_parts, dy_parts):
        rows = x_part.shape[0]
        x_ref[at : at + rows, :] = x_part[...]
        dy_ref[at : at + rows, :] = dy_part[...]
        at += rows
    x = x_ref[...]
    acc_g[...] += dot(x, gate_ref[...])
    acc_u[...] += dot(x, up_ref[...])
    acc_b[...] += lax.dot_general(dy_ref[...], down_ref[...], BY_LAST, preferred_element_type=F32)

    @pl.when(step == pl.num_programs(0) - 1)
    def _():
        pre_gate, pre_up, back = acc_g[...], acc_u[...], acc_b[...]
        part = pre_gate.shape[1]
        sigma = jax.nn.sigmoid(pre_gate)
        act = pre_gate * sigma
        hidden = act * pre_up
        prob = jnp.sum(hidden * back, axis=1, keepdims=True)
        prob_ref[...] = jnp.broadcast_to(prob, prob_ref.shape).astype(BF)
        grad_g = back * pre_up * sigma * (1.0 + pre_gate * (1.0 - sigma))
        grad_u = back * act
        grads_ref[:, :part] = grad_g.astype(BF)
        grads_ref[:, part:] = grad_u.astype(BF)
        grads_t_ref[:part, :] = grad_g.T.astype(BF)
        grads_t_ref[part:, :] = grad_u.T.astype(BF)
        hidden_t_ref[...] = hidden.T.astype(BF)


def forward(parts, gate_w, up_w, down_w, after, pin, mib):
    width, part = gate_w.shape
    count = sum(p.shape[0] for p in parts)
    block = 1024
    steps = width // block
    pinned = (*parts, *parts, gate_w, up_w, down_w)
    if pin:
        pinned = in_hbm(*pinned)
    return pl.pallas_call(
        functools.partial(forward_kernel, len(parts)),
        grid=(steps,),
        in_specs=[pl.BlockSpec((p.shape[0], block), lambda i: (0, i)) for p in parts]
        + [pl.BlockSpec((p.shape[0], block), lambda i: (0, i + steps)) for p in parts]
        + [
            pl.BlockSpec((block, part), lambda i: (i, 0)),
            pl.BlockSpec((block, part), lambda i: (i, 0)),
            pl.BlockSpec((part, block), lambda i: (0, i)),
        ]
        + [pl.BlockSpec(memory_space=pl.ANY)] * len(after),
        out_specs=[
            pl.BlockSpec((count, block), lambda i: (0, i)),
            pl.BlockSpec((count, block), lambda i: (0, i)),
            pl.BlockSpec((count, 2 * part), lambda i: (0, 0)),
            pl.BlockSpec((2 * part, count), lambda i: (0, 0)),
            pl.BlockSpec((part, count), lambda i: (0, 0)),
            pl.BlockSpec((count, LANES), lambda i: (0, 0)),
        ],
        out_shape=[
            pltpu.HBM((count, width), BF),
            pltpu.HBM((count, width), BF),
            pltpu.HBM((count, 2 * part), BF),
            pltpu.HBM((2 * part, count), BF),
            pltpu.HBM((part, count), BF),
            pltpu.HBM((count, LANES), BF),
        ],
        scratch_shapes=[pltpu.VMEM((count, part), F32)] * 3,
        compiler_params=limit(mib),
        cost_estimate=cost(6 * count * width * part, 6 * width * part + 8 * count * width),
    )(*pinned, *after)


def weight_kernel(groups, own, at_ref, *refs):
    x_refs, dy_refs = refs[:groups], refs[groups : 2 * groups]
    g_refs, h_refs = refs[2 * groups : 3 * groups], refs[3 * groups : 4 * groups]
    out_refs, (turned, tall_x, tall_dy) = refs[-5:-3], refs[-3:]
    both = g_refs[0].shape[0]

    @pl.when((pl.program_id(0) == 0) & (pl.program_id(1) == 0))
    def _():
        at = 0
        for g, h in zip(g_refs, h_refs):
            rows = g.shape[1]
            turned[:both, at : at + rows] = g[...]
            turned[both:, at : at + rows] = h[...]
            at += rows

    at = 0
    for x, dy in zip(x_refs, dy_refs):
        rows = x.shape[0]
        tall_x[at : at + rows, :] = x[...]
        tall_dy[at : at + rows, :] = dy[...]
        at += rows
    top = dot(turned[:both, :], tall_x[...]).astype(BF)
    low = dot(turned[both:, :], tall_dy[...]).astype(BF)
    if own:
        sent = pl.program_id(0) < 2

        @pl.when(sent)
        def _():
            out_refs[0][0, :both, :] = top
            out_refs[0][0, both:, :] = low

        @pl.when(jnp.logical_not(sent))
        def _():
            out_refs[1][:both, :] = top
            out_refs[1][both:, :] = low
    else:
        half = out_refs[0].shape[1]
        out_refs[0][0] = top[:half]
        out_refs[1][0, : both - half, :] = top[half:]
        out_refs[1][0, both - half :, :] = low


def weight_blocks(at, slice_w, xs, dys, grads_t, hiddens_t, own, after=()):
    block = 512 if own else 256
    steps = slice_w // block
    count = at.shape[0]
    rows = grads_t[0].shape[0] + hiddens_t[0].shape[0]
    total = sum(v.shape[0] for v in xs)
    tall = [pl.BlockSpec((v.shape[0], block), lambda k, i, at: (0, at[k] * steps + i)) for v in xs]
    whole = [pl.BlockSpec(v.shape, lambda k, i, at: (0, 0)) for v in (*grads_t, *hiddens_t)]
    if own:
        last = steps - 1
        out_specs = [
            pl.BlockSpec(
                (1, rows, block),
                lambda k, i, at: (jnp.minimum(k, 1), 0, jnp.where(k < 2, i, last)),
            ),
            pl.BlockSpec((rows, block), lambda k, i, at: (0, jnp.where(k < 2, 0, i))),
        ]
        out_shape = [
            jax.ShapeDtypeStruct((2, rows, slice_w), BF),
            pltpu.HBM((rows, slice_w), BF),
        ]
    else:
        out_specs = [pl.BlockSpec((1, rows // 2, block), lambda k, i, at: (k, 0, i))] * 2
        out_shape = [jax.ShapeDtypeStruct((count, rows // 2, slice_w), BF)] * 2
    return pl.pallas_call(
        functools.partial(weight_kernel, len(xs), own),
        grid_spec=pltpu.PrefetchScalarGridSpec(
            num_scalar_prefetch=1,
            grid=(count, steps),
            in_specs=tall + tall + whole + [pl.BlockSpec(memory_space=pl.ANY)] * len(after),
            out_specs=out_specs,
            scratch_shapes=[
                pltpu.VMEM((rows, total), BF),
                pltpu.VMEM((total, block), BF),
                pltpu.VMEM((total, block), BF),
            ],
        ),
        out_shape=out_shape,
        compiler_params=limit(20),
        cost_estimate=cost(count * 2 * rows * slice_w * total, count * 7 * MIB),
    )(at, *in_hbm(*xs, *dys, *grads_t, *hiddens_t), *after)


def join_kernel(a_ref, b_ref, *refs):
    out_ref = refs[-1]
    rows = a_ref.shape[0]
    out_ref[:rows, :] = a_ref[...]
    out_ref[rows:, :] = b_ref[...]


def join_rows(a, b, after):
    block = 2048
    spec = pl.BlockSpec((a.shape[0], block), lambda i: (0, i))
    return pl.pallas_call(
        join_kernel,
        grid=(a.shape[1] // block,),
        in_specs=[spec, spec] + [pl.BlockSpec(memory_space=pl.ANY)] * len(after),
        out_specs=pl.BlockSpec((2 * a.shape[0], block), lambda i: (0, i)),
        out_shape=jax.ShapeDtypeStruct((2 * a.shape[0], a.shape[1]), BF),
        compiler_params=limit(8),
        cost_estimate=cost(0, 8 * a.size),
    )(a, b, *after)


def join_far_kernel(cut, near_l, near_r, pair_l, pair_r, far_l, far_r):
    step = near_l.shape[0]
    far_l[:cut, :] = near_l[:cut]
    far_l[cut:, :] = pair_l[:step]
    far_r[: step - cut, :] = near_r[cut:]
    far_r[step - cut :, :] = pair_r[step:]


def join_far(near_l, near_r, pair_l, pair_r, cut):
    step, width = near_l.shape
    block = 2048
    parts = (near_l, near_r, pair_l, pair_r)
    sizes = (cut + step, 2 * step - cut)
    return pl.pallas_call(
        functools.partial(join_far_kernel, cut),
        grid=(width // block,),
        in_specs=[pl.BlockSpec((p.shape[0], block), lambda i: (0, i)) for p in parts],
        out_specs=[pl.BlockSpec((n, block), lambda i: (0, i)) for n in sizes],
        out_shape=[jax.ShapeDtypeStruct((n, width), BF) for n in sizes],
        compiler_params=limit(8),
        cost_estimate=cost(0, 12 * step * width),
    )(*parts)


def pass_kernel(*refs):
    pass


def order(value, after):
    spec = pl.BlockSpec(memory_space=pl.ANY)
    return pl.pallas_call(
        pass_kernel,
        in_specs=[spec] * (1 + len(after)),
        out_specs=spec,
        out_shape=jax.ShapeDtypeStruct(value.shape, value.dtype),
        input_output_aliases={0: 0},
        cost_estimate=cost(0, 0),
    )(value, *after)


def add_rows(a, b):
    return (a.astype(F32) + b.astype(F32)).astype(BF)


def dp_add_kernel(rest_ref, far_a_ref, far_b_ref, *refs):
    right_ref, left_ref = refs[-2:]
    half = far_a_ref.shape[0]
    right_ref[:half, :] = add_rows(rest_ref[0, :half], far_a_ref[...])
    right_ref[half:, :] = rest_ref[0, half:]
    left_ref[:half, :] = rest_ref[1, :half]
    left_ref[half:, :] = add_rows(rest_ref[1, half:], far_b_ref[...])


def dp_add(rest, far_a, far_b, after):
    _, rows, width = rest.shape
    block = 256
    spec = pl.BlockSpec((rows // 2, block), lambda i: (0, i))
    out = pl.BlockSpec((rows, block), lambda i: (0, i))
    return pl.pallas_call(
        dp_add_kernel,
        grid=(width // block,),
        in_specs=[pl.BlockSpec((2, rows, block), lambda i: (0, 0, i)), spec, spec]
        + [pl.BlockSpec(memory_space=pl.ANY)] * len(after),
        out_specs=[out, out],
        out_shape=[jax.ShapeDtypeStruct((rows, width), BF)] * 2,
        compiler_params=limit(12),
        cost_estimate=cost(2 * rows * width, 10 * rows * width),
    )(rest, far_a, far_b, *after)


def etp_add_kernel(to_left, to_right, left_ref, right_ref, far_a_ref, far_b_ref, *refs):
    left_out, right_out = refs[-2:]
    right_out[...] = right_ref[...]
    left_out[...] = left_ref[...]
    for at, source, rows in to_right:
        right_out[at : at + rows, :] = add_rows(right_ref[at : at + rows], far_a_ref[source : source + rows])
    for at, source, rows in to_left:
        left_out[at : at + rows, :] = add_rows(left_ref[at : at + rows], far_b_ref[source : source + rows])


def etp_add(to_left, to_right, left, right, far_a, far_b, after):
    rows, width = left.shape
    block = 11 * LANES
    parts = (left, right, far_a, far_b)
    spec = pl.BlockSpec((rows, block), lambda i: (0, i))
    return pl.pallas_call(
        functools.partial(etp_add_kernel, to_left, to_right),
        grid=(width // block,),
        in_specs=[pl.BlockSpec((p.shape[0], block), lambda i: (0, i)) for p in parts]
        + [pl.BlockSpec(memory_space=pl.ANY)] * len(after),
        out_specs=[spec, spec],
        out_shape=[jax.ShapeDtypeStruct((rows, width), BF)] * 2,
        compiler_params=limit(12),
        cost_estimate=cost(rows * width, 10 * rows * width),
    )(*parts, *after)


def dx_kernel(sources, bands, *refs):
    grads, probs = refs[:sources], refs[sources : 2 * sources]
    gate_ref, up_ref = refs[2 * sources : 2 * sources + 2]
    out_refs, lhs, sums = refs[-len(bands) - 2 : -2], refs[-2], refs[-1]

    @pl.when(pl.program_id(0) == 0)
    def _():
        at = 0
        for grad, prob in zip(grads, probs):
            rows = grad.shape[0]
            lhs[at : at + rows, :] = grad[...]
            sums[at : at + rows, :] = prob[...]
            at += rows

    part = gate_ref.shape[1]
    total = lax.dot_general(lhs[:, :part], gate_ref[...], BY_LAST, preferred_element_type=F32)
    total += lax.dot_general(lhs[:, part:], up_ref[...], BY_LAST, preferred_element_type=F32)
    total = total.astype(BF)
    for out, band in zip(out_refs, bands):
        to = 0
        for at, rows in band:
            out[to : to + rows, :] = total[at : at + rows]
            to += rows

    @pl.when(pl.program_id(0) == pl.num_programs(0) - 1)
    def _():
        for out, band in zip(out_refs, bands):
            to = 0
            for at, rows in band:
                out[to : to + rows, out.shape[1] - LANES :] = sums[at : at + rows, :]
                to += rows


def dx_blocks(grads, probs, gate_w, up_w, bands, after):
    width, part = gate_w.shape
    count = sum(g.shape[0] for g in grads)
    block = 11 * LANES
    steps = (width + LANES) // block
    sizes = [sum(rows for _, rows in band) for band in bands]
    return pl.pallas_call(
        functools.partial(dx_kernel, len(grads), bands),
        grid=(steps,),
        in_specs=[pl.BlockSpec(v.shape, lambda i: (0, 0)) for v in (*grads, *probs)]
        + [pl.BlockSpec((block, part), lambda i: (i, 0))] * 2
        + [pl.BlockSpec(memory_space=pl.ANY)] * len(after),
        out_specs=[pl.BlockSpec((rows, block), lambda i: (0, i)) for rows in sizes],
        out_shape=[jax.ShapeDtypeStruct((rows, width + LANES), BF) for rows in sizes],
        scratch_shapes=[pltpu.VMEM((count, 2 * part), BF), pltpu.VMEM((count, LANES), BF)],
        compiler_params=limit(20),
        cost_estimate=cost(4 * count * width * part, 4 * width * part + 2 * count * width),
    )(*grads, *probs, gate_w, up_w, *after)


def final_kernel(own_ref, left_ref, right_ref, *refs):
    gate_ref, up_ref, down_ref = refs[-3:]
    total = own_ref[...].astype(F32) + left_ref[...].astype(F32) + right_ref[...].astype(F32)
    part = down_ref.shape[0]
    gate_ref[...] = total[:part].T.astype(BF)
    up_ref[...] = total[part : 2 * part].T.astype(BF)
    down_ref[...] = total[2 * part :].astype(BF)


def final_sum(own, left, right, after):
    rows, width = left.shape
    part = rows // 3
    block = 256
    spec = pl.BlockSpec((rows, block), lambda i: (0, i))
    tall = pl.BlockSpec((block, part), lambda i: (i, 0))
    return pl.pallas_call(
        final_kernel,
        grid=(width // block,),
        in_specs=[spec] * 3
        + [pl.BlockSpec(memory_space=pl.ANY)] * len(after),
        out_specs=[tall, tall, pl.BlockSpec((part, block), lambda i: (0, i))],
        out_shape=[jax.ShapeDtypeStruct((width, part), BF)] * 2 + [jax.ShapeDtypeStruct((part, width), BF)],
        compiler_params=limit(16),
        cost_estimate=cost(rows * width, 8 * rows * width),
    )(*in_hbm(own), left, right, *after)


def ring(axis):
    size = lax.axis_size(axis)
    return [(i, (i + 1) % size) for i in range(size)], [(i, (i - 1) % size) for i in range(size)]


def ring_first(far_a, far_b, axis):
    to_right, to_left = ring(axis)
    return lax.ppermute(far_a, axis, to_right), lax.ppermute(far_b, axis, to_left)


def ring_second(left, right, axis):
    to_right, to_left = ring(axis)
    return lax.ppermute(right, axis, to_right), lax.ppermute(left, axis, to_left)


def body(inputs, upstream, experts, gate_probs, gate_weight, up_weight, down_weight):
    experts_n = lax.axis_size("ep")
    layers = experts_n // 2
    width = inputs.shape[1]
    me = lax.axis_index("ep")
    z, core = me // 2, me % 2
    expert_ids = jnp.stack(
        [2 * ((z + dz) % layers) + (core ^ dc) for dc in range(2) for dz in range(layers)]
    ).astype(jnp.int32)
    swap = [(2 * i + j, 2 * i + 1 - j) for i in range(layers) for j in range(2)]

    def shift(dz):
        return [(2 * i + j, 2 * ((i + dz) % layers) + j) for i in range(layers) for j in range(2)]

    onehot, chosen, slot_gate = slot_tables(experts, gate_probs, expert_ids, CAP)
    slots = experts_n * CAP
    pick = onehot.astype(BF).reshape(slots, -1)
    gate = slot_gate.astype(BF).astype(F32).reshape(slots, 1)
    mine, others = pick_rows(pick, gate, inputs, upstream)
    others = lax.ppermute(others, "ep", swap)

    gate_w, up_w, down_w = gate_weight[0], up_weight[0], down_weight[0]
    blocks = {}
    for dz in range(layers):
        at = slice(dz * CAP, (dz + 1) * CAP)
        block = jnp.concatenate([mine[at], others[at]])
        if dz == 2:
            block = order(block, (blocks[1],))
        blocks[dz] = lax.ppermute(block, "ep", shift(dz)) if dz else block
    step = 2 * CAP
    weights = (gate_w, up_w, down_w)
    to_right, to_left = ring("etp")
    cut = 32
    near = blocks[0]
    near_l, near_r = lax.ppermute(near, "etp", to_right), lax.ppermute(near, "etp", to_left)
    pair = join_rows(blocks[1], blocks[3], (near_l, near_r))
    pair_l, pair_r = lax.ppermute(pair, "etp", to_right), lax.ppermute(pair, "etp", to_left)
    far_l, far_r = join_far(near_l, near_r, pair_l, pair_r, cut)
    far_l, far_r = lax.ppermute(far_l, "etp", to_right), lax.ppermute(far_r, "etp", to_left)
    first = forward([near, near_l, near_r, pair, pair_l, pair_r], *weights, (), True, 28)

    last = blocks[2]
    last_l, last_r = lax.ppermute(last, "etp", to_right), lax.ppermute(last, "etp", to_left)
    second = forward([last, last_l, last_r], *weights, first[-1:], True, 20)
    last_l, last_r = order(last_l, second[-1:]), order(last_r, second[-1:])
    last_fl = lax.ppermute(last_l[: step - cut], "etp", to_right)
    last_fr = lax.ppermute(last_r[step - cut :], "etp", to_left)
    bands = [[(k * step, step), ((3 + 2 * k) * step, 2 * step)] for k in range(3)]
    bands += [[((9 + k) * step, step)] for k in range(3)]
    sources = [first[2], second[2]], [first[5], second[5]]
    own_p, left_p, right_p, own_q, left_q, right_q = dx_blocks(*sources, gate_w, up_w, bands, ())
    third = forward([far_l, far_r, last_fl, last_fr], *weights, (own_p,), False, 16)
    xs, dys, _, grads_t, hiddens_t, _ = zip(first, second, third)

    dp = lax.axis_size("dp")
    slice_w = width // dp
    my_dp = lax.axis_index("dp")

    def weights_for(ahead, own, after=()):
        at = jnp.stack([(my_dp + k) % dp for k in ahead]).astype(jnp.int32)
        return weight_blocks(at, slice_w, xs, dys, grads_t, hiddens_t, own, after)

    far_a, far_b = weights_for((2,), False)
    got_wa, got_wb = ring_first(far_a[0], far_b[0], "dp")
    wide = cut + step
    more = 3 * step - wide
    bands = [[(0, wide), (3 * step, step - cut)], [(wide, more), (4 * step - cut, cut)]]
    far_l, far_r = dx_blocks([third[2]], [third[5]], gate_w, up_w, bands, (far_a,))
    got_l, got_r = ring_first(far_l, far_r, "etp")

    rest, own_w = weights_for((1, dp - 1, 0), True, (far_l,))
    plan_p = [(cut, 0, step - cut), (2 * step, step - cut, step)], [(0, 0, cut), (step, cut, step)]
    plan_q = [(step - cut, more, cut)], [(0, wide, step - cut)]
    left_q, right_q = etp_add(*plan_q, left_q, right_q, got_l, got_r, (rest,))
    left_p, right_p = etp_add(*plan_p, left_p, right_p, got_l, got_r, (rest,))
    right_w, left_w = dp_add(rest, got_wa, got_wb, (left_q, left_p))
    from_left_w, from_right_w = ring_second(left_w, right_w, "dp")

    returned = {}
    for members, own, left, right in [((2,), own_q, left_q, right_q), ((0, 1, 3), own_p, left_p, right_p)]:
        from_left, from_right = ring_second(left, right, "etp")
        from_left = order(from_left, (right_w,))
        total = (own.astype(F32) + from_left.astype(F32) + from_right.astype(F32)).astype(BF)
        for i, dz in enumerate(members):
            block = total[i * step : (i + 1) * step]
            returned[dz] = lax.ppermute(block, "ep", shift(layers - dz)) if dz else block
    mine_rows = jnp.concatenate([returned[dz][:CAP] for dz in range(layers)])
    others = jnp.concatenate([returned[dz][CAP:] for dz in range(layers)])
    others = lax.ppermute(others, "ep", swap)
    dx_slots = jnp.concatenate([mine_rows, others])
    grad_inputs = lax.dot_general(pick, dx_slots[:, :width], BY_FIRST, preferred_element_type=F32).astype(BF)
    prob_sum = dx_slots[:, width].astype(F32).reshape(experts_n, CAP)
    gates = gate.reshape(experts_n, CAP)
    prob_slots = (prob_sum / jnp.where(gates > 0, gates, 1.0)).astype(BF).astype(F32)
    per_expert = jnp.sum(jnp.where(onehot, prob_slots[:, :, None], 0.0), axis=1)
    grad_probs = jnp.sum(jnp.where(chosen, per_expert.T[:, None, :], 0.0), axis=2)

    grad_gate, grad_up, grad_down = final_sum(own_w, from_left_w, from_right_w, (grad_inputs,))
    return (grad_inputs, grad_probs, grad_gate[None], grad_up[None], grad_down[None])


def solution(mesh):
    tokens = P(("ep", "etp", "dp"), None)
    return jax.shard_map(
        body,
        mesh=mesh,
        in_specs=(tokens, tokens, tokens, tokens, P("ep", None, "etp"), P("ep", None, "etp"), P("ep", "etp", None)),
        out_specs=(tokens, tokens, P("ep", "dp", "etp"), P("ep", "dp", "etp"), P("ep", "etp", "dp")),
        check_vma=False,
    )
```
